128 devices in a mesh: dp: 32 (over x, y, core), rep: 4 (over z).
Axes of the slice: x: 4, y: 4, z: 4, core: 2. Of those that a mesh axis runs over, the one named last changes fastest.
Arguments:
- frames: bfloat16 [2048, 4, 16, 4096], P('dp', 'rep'), may hold values from -6 to 6
- clip_lengths: int32 [32, 4, 4], P('dp', 'rep'), may hold values from 1 to 912, as said below
- block_dest: int32 [32, 4, 2, 64], P('dp', 'rep'), may hold values from -1 to 31, as said below
- frame_codes: int32 [2048, 4, 16], P('dp', 'rep'), may hold values from 0 to 1023
- codebook: bfloat16 [1024, 128], replicated, may hold values from -4 to 4
- encoder_weight: bfloat16 [4096, 512], replicated, may hold values from -0.09375 to 0.09375
- latent_weight: bfloat16 [512, 128], replicated, may hold values from -0.25 to 0.25
- expand_weight: bfloat16 [512, 128], replicated, may hold values from -0.5 to 0.5
- decoder_weight: bfloat16 [512, 4096], replicated, may hold values from -0.25 to 0.25
Outputs:
- latents: float32 [1024, 4, 16, 128], P('dp', 'rep')
- grad_encoder: float32 [4096, 512], P(('dp', 'rep'))
- grad_latent: float32 [512, 128], P(('dp', 'rep'))
- grad_expand: float32 [512, 128], P(('dp', 'rep'))
- grad_decoder: float32 [512, 4096], P(('dp', 'rep'))
The draws below stay inside these ranges and needn't reach their ends.
Inputs may be any that keep to these rules, and one draw needn't show every extreme that they name: `clip_lengths`: each device's clips take ceil(length / 16) slots each; one device uses between 4 and 60 slots, some device of each rep index exactly 60, and the devices of one rep index use 32 slots each on average. `block_dest`: row 0 is the receiving dp index (same rep index), row 1 the receiving slot, both -1 exactly for the slots that no clip uses. Every device receives exactly 32 blocks, one into each slot, and at most 2 blocks from any one device; some device sends 2 blocks to one device.
All inputs are finite; a program needn't handle non-finite values.
Results may differ from the reference program's by a relative error of at most 0.0059.
Values may be sent and summed in bfloat16 or wider, within the bound.
No kernel may reach another device: no remote copies, remote signals or barrier semaphores. Data moves between devices by JAX's collectives and lax.ppermute only.
A program may use at most 128 MiB of HBM per device.

```python
import jax
import jax.numpy as jnp
from jax import lax

FEAT = 4096
HID = 512
LAT = 128
CODES = 1024
BLK = 16
NB = 64
CLIPS = 4
RB = 32
N_DP = 32
N_REP = 4


def clip_plan(key):
    subkeys = jax.random.split(key, 5)
    pair_count = N_DP // 2
    spread = jax.random.randint(subkeys[0], (N_REP, pair_count), 0, RB - CLIPS + 1, dtype=jnp.int32)
    spread = spread.at[:, 0].set(RB - CLIPS)
    paired = jnp.stack([RB + spread, RB - spread], axis=-1).reshape(N_REP, N_DP)
    shuffle = jax.vmap(lambda single: jax.random.permutation(single, N_DP))(jax.random.split(subkeys[1], N_REP)).astype(jnp.int32)
    counts = jnp.take_along_axis(paired, shuffle, axis=1)
    fullest = (counts == 2 * RB - CLIPS)[:, :, None]
    limit = (counts - CLIPS + 1)[:, :, None]
    cut_points = jax.random.randint(subkeys[2], (N_REP, N_DP, CLIPS - 1), 0, limit, dtype=jnp.int32)
    cut_points = jnp.sort(cut_points, axis=-1)
    cut_points = jnp.where(fullest, 0, cut_points)
    zero_col = jnp.zeros((N_REP, N_DP, 1), jnp.int32)
    edges = jnp.concatenate([zero_col, cut_points, (counts - CLIPS)[:, :, None]], axis=-1)
    blocks = jnp.diff(edges, axis=-1) + 1
    tails = jax.random.randint(subkeys[3], (N_REP, N_DP, CLIPS), 1, BLK + 1, dtype=jnp.int32)
    clip_index = jnp.arange(CLIPS, dtype=jnp.int32)[None, None, :]
    tails = jnp.where(fullest & (clip_index == 0), 1, tails)
    tails = jnp.where(fullest & (clip_index == CLIPS - 1), BLK, tails)
    lengths = (blocks - 1) * BLK + tails
    starts = jnp.cumsum(counts, axis=1) - counts
    slot_index = jnp.arange(NB, dtype=jnp.int32)
    global_index = starts[:, :, None] + slot_index[None, None, :]
    live_slot = slot_index[None, None, :] < counts[:, :, None]
    owners = jax.vmap(lambda single: jax.random.permutation(single, N_DP))(jax.random.split(subkeys[4], N_REP)).astype(jnp.int32)
    device = jax.vmap(lambda owner_row, index_rows: owner_row[index_rows])(owners, global_index % N_DP)
    target = jnp.where(live_slot, device, -1)
    place = jnp.where(live_slot, global_index // N_DP, -1)
    dest = jnp.stack([target, place], axis=2).astype(jnp.int32)
    return (lengths.transpose(1, 0, 2).astype(jnp.int32), dest.transpose(1, 0, 2, 3))


def draw_clip_lengths(key, part):
    return clip_plan(key)[0]


def draw_block_dest(key, part):
    return clip_plan(key)[1]


def place_ends(values, stream_key, low, top_value):
    longest = values.shape.index(max(values.shape))
    spots = []
    for shift in (0, 1):
        where = [jax.random.randint(jax.random.fold_in(stream_key, axis), (), 0, length) for axis, length in enumerate(values.shape)]
        where[longest] = (where[longest] + shift) % values.shape[longest]
        spots.append(tuple(where))
    return values.at[spots[0]].set(low).at[spots[1]].set(top_value)


def steps_of(rng, dims, cuts, smallest, top_value):
    factor_of = 1.0
    for dim, blocks in cuts:
        draws = jax.random.uniform(jax.random.fold_in(jax.random.fold_in(rng, 6), dim), (blocks,), jnp.float32, smallest / len(cuts), top_value / len(cuts))
        factor_of = factor_of * jnp.repeat(jnp.exp(draws), dims[dim] // blocks).reshape((-1,) + (1,) * (len(dims) - 1 - dim))
    return factor_of


def normal_values(rng, dims, scale, reach, shards=(), kind=jnp.bfloat16):
    drawn = scale * jax.random.normal(rng, dims, jnp.float32)
    if shards:
        drawn = drawn * steps_of(rng, dims, shards, -0.22, 0.18)
    return jnp.clip(drawn, -reach, reach).astype(kind)


def setup_inputs(seed: int = 0) -> dict:
    key_of = jax.random.split(jax.random.key(seed), 10)
    frames = normal_values(key_of[0], (N_DP * NB, N_REP, BLK, FEAT), 1.0, 6.0, ((0, 32), (1, 4)))
    clip_lengths = draw_clip_lengths(jax.random.fold_in(key_of[9], 71), 0)
    block_dest = draw_block_dest(jax.random.fold_in(key_of[9], 71), 0)
    frame_codes = place_ends(jax.random.randint(key_of[3], (N_DP * NB, N_REP, BLK), 0, CODES), jax.random.fold_in(key_of[3], 1), 0, CODES - 1).astype(jnp.int32)
    codebook = normal_values(key_of[4], (CODES, LAT), 0.7, 4.0)
    encoder_weight = normal_values(key_of[5], (FEAT, HID), FEAT ** -0.5, 0.09375)
    latent_weight = normal_values(key_of[6], (HID, LAT), HID ** -0.5, 0.25)
    expand_weight = normal_values(key_of[7], (HID, LAT), LAT ** -0.5, 0.5)
    decoder_weight = normal_values(key_of[8], (HID, FEAT), HID ** -0.5, 0.25)
    return dict(frames=frames, clip_lengths=clip_lengths, block_dest=block_dest, frame_codes=frame_codes, codebook=codebook, encoder_weight=encoder_weight, latent_weight=latent_weight, expand_weight=expand_weight, decoder_weight=decoder_weight)


def elu_slope(values):
    return jnp.where(values > 0, 1.0, jnp.exp(jnp.minimum(values, 0.0)))


def across_rows(left, right):
    return lax.dot_general(left, right, (((0,), (0,)), ((), ())), preferred_element_type=jnp.float32)


def against_rows(left, right):
    return lax.dot_general(left, right, (((1,), (1,)), ((), ())), preferred_element_type=jnp.float32)


def row_lengths(lengths):
    blocks = (lengths + BLK - 1) // BLK
    ends = jnp.cumsum(blocks, axis=-1)
    starts = ends - blocks
    position = jnp.arange(NB * BLK, dtype=jnp.int32)
    slot_index = position // BLK
    member = (slot_index >= starts[..., None] * 1) & (slot_index < ends[..., None])
    offset = position - starts[..., None] * BLK
    valid = member & (offset < lengths[..., None])
    counted = jnp.sum(jnp.where(valid, lengths[..., None], 0), axis=-2).astype(jnp.int32)
    return counted.reshape(lengths.shape[:-1] + (NB, BLK))


def train_rows(placed, row_codes, row_length, codebook, encoder_weight, latent_weight, expand_weight, decoder_weight, reduce_decoder):
    pre_hidden = jnp.dot(placed, encoder_weight, preferred_element_type=jnp.float32)
    hidden = jax.nn.elu(pre_hidden).astype(jnp.bfloat16)
    latents = jnp.dot(hidden, latent_weight, preferred_element_type=jnp.float32)
    quantized = jnp.take(codebook, row_codes, axis=0)
    pre_decoded = against_rows(quantized, expand_weight)
    decoded = jax.nn.elu(pre_decoded).astype(jnp.bfloat16)
    restored = jnp.dot(decoded, decoder_weight, preferred_element_type=jnp.float32)
    frame_weight = jnp.where(row_length > 0, 1.0 / jnp.maximum(row_length, 1).astype(jnp.float32), 0.0)[:, None]
    out_grad = (2.0 * frame_weight * (restored - placed.astype(jnp.float32))).astype(jnp.bfloat16)
    grad_decoder = across_rows(decoded, out_grad)
    back_decoded = (against_rows(out_grad, decoder_weight) * elu_slope(pre_decoded)).astype(jnp.bfloat16)
    grad_expand = across_rows(back_decoded, quantized)
    decoder_part = reduce_decoder(grad_decoder, grad_expand)
    latent_grad = (jnp.dot(back_decoded, expand_weight, preferred_element_type=jnp.float32)
                   + 2.0 * frame_weight * (latents - quantized.astype(jnp.float32))).astype(jnp.bfloat16)
    grad_latent = across_rows(hidden, latent_grad)
    back_hidden = (against_rows(latent_grad, latent_weight) * elu_slope(pre_hidden)).astype(jnp.bfloat16)
    grad_encoder = across_rows(placed, back_hidden)
    return latents, decoder_part, grad_latent, grad_encoder


def pair_up(first, second):
    return first, second


def reference(frames, clip_lengths, block_dest, frame_codes, codebook, encoder_weight, latent_weight, expand_weight, decoder_weight):
    length_rows = row_lengths(clip_lengths)
    target = block_dest[:, :, 0, :]
    place = block_dest[:, :, 1, :]
    flat_target = jnp.where(target >= 0, target * RB + place, N_DP * RB).astype(jnp.int32)
    rep_index = jnp.arange(N_REP, dtype=jnp.int32)[None, :, None]
    frames_by_slot = frames.reshape(N_DP, NB, N_REP, BLK, FEAT).transpose(0, 2, 1, 3, 4)
    codes_by_slot = frame_codes.reshape(N_DP, NB, N_REP, BLK).transpose(0, 2, 1, 3)
    placed = jnp.zeros((N_DP * RB, N_REP, BLK, FEAT), frames.dtype).at[flat_target, rep_index].set(frames_by_slot, mode="drop")
    placed_codes = jnp.zeros((N_DP * RB, N_REP, BLK), jnp.int32).at[flat_target, rep_index].set(codes_by_slot, mode="drop")
    placed_length = jnp.zeros((N_DP * RB, N_REP, BLK), jnp.int32).at[flat_target, rep_index].set(length_rows, mode="drop")
    device_frames = placed.reshape(N_DP, RB, N_REP, BLK, FEAT).transpose(0, 2, 1, 3, 4).reshape(N_DP * N_REP, RB * BLK, FEAT)
    device_codes = placed_codes.reshape(N_DP, RB, N_REP, BLK).transpose(0, 2, 1, 3).reshape(N_DP * N_REP, RB * BLK)
    device_length = placed_length.reshape(N_DP, RB, N_REP, BLK).transpose(0, 2, 1, 3).reshape(N_DP * N_REP, RB * BLK)

    def device_step(carry, pieces):
        latents, decoder_part, grad_latent, grad_encoder = train_rows(pieces[0], pieces[1], pieces[2], codebook, encoder_weight, latent_weight, expand_weight, decoder_weight, pair_up)
        updated = (carry[0] + grad_encoder, carry[1] + grad_latent, carry[2] + decoder_part[1], carry[3] + decoder_part[0])
        return updated, latents

    start = (jnp.zeros((FEAT, HID), jnp.float32), jnp.zeros((HID, LAT), jnp.float32),
             jnp.zeros((HID, LAT), jnp.float32), jnp.zeros((HID, FEAT), jnp.float32))
    totals, latent_rows = lax.scan(device_step, start, (device_frames, device_codes, device_length))
    latents = latent_rows.reshape(N_DP, N_REP, RB, BLK, LAT).transpose(0, 2, 1, 3, 4).reshape(N_DP * RB, N_REP, BLK, LAT)
    return latents, totals[0], totals[1], totals[2], totals[3]
```

```python
import functools

import jax
import jax.numpy as jnp
from jax import lax
from jax.experimental import pallas as pl
from jax.experimental.pallas import tpu as pltpu
from jax.sharding import PartitionSpec as P

BLK = 16
NB = 64
RB = 32
FEAT = 4096
HID = 512
LAT = 128
CODES = 1024
ROWS = NB * BLK
PEERS = 32
META = 2 * BLK + 8
DROWS = 136
TILE = 512
STEPS = FEAT // TILE
BF = jnp.bfloat16
F32 = jnp.float32
LEN, X, Y, C, Z = 0, 4, 5, 6, 7


def dot(left, right, lc, rc):
    return lax.dot_general(left, right, (((lc,), (rc,)), ((), ())), preferred_element_type=F32)


def slope_of(values):
    return jnp.exp(jnp.minimum(values, 0.0))


def iota(shape, dim):
    return lax.broadcasted_iota(jnp.int32, shape, dim)


def double_weight(scal):
    position = iota((ROWS, 1), 0)
    weight = jnp.zeros((ROWS, 1), F32)
    start = 0
    for clip in range(4):
        length = scal[LEN + clip]
        span = (length + (BLK - 1)) // BLK * BLK
        inside = (position >= start) & (position < start + length)
        share = 2.0 / jnp.full((ROWS, 1), length, jnp.int32).astype(F32)
        weight = jnp.where(inside, share, weight)
        start = start + span
    return weight


def dest_of(rank, scal):
    half, first, second, depth = rank // 64, rank // 16 % 4, rank // 4 % 4, rank % 4
    core = jnp.where(half == 0, 1 - scal[C], scal[C])
    col = (scal[X] + jnp.where(core == 0, first, second)) % 4
    row = (scal[Y] + jnp.where(core == 0, second, first)) % 4
    return ((col * 4 + row) * 2 + core) * 4 + (scal[Z] + depth) % 4


def decoder_kernel(scal, codes, codebook, expand, x, wd, og, send, keep, q_out, decoded, dec_t, w2):
    @pl.when(pl.program_id(0) == 0)
    def _():
        hot = (iota((CODES, ROWS), 0) == codes[...]).astype(BF)
        q_t = dot(codebook[...], hot, 0, 0).astype(BF)
        q = q_t.astype(F32).T.astype(BF)
        q_out[...] = q
        pre = dot(q, expand[...], 1, 1)
        decoded[...] = jnp.where(pre > 0, pre, slope_of(pre) - 1.0).astype(BF)
        source = iota((HID, 1), 0)
        source = dest_of(source // 4, scal) * 4 + source % 4
        moved = dot((iota((HID, HID), 1) == source).astype(BF), expand[...], 1, 0).astype(BF)
        pre = dot(moved, q_t, 1, 0)
        dec_t[...] = jnp.where(pre > 0, pre, slope_of(pre) - 1.0).astype(BF)
        w2[...] = double_weight(scal)

    restored = dot(decoded[...], wd[...], 1, 0)
    grad = (w2[...] * (restored - x[...].astype(F32))).astype(BF)
    og[...] = grad
    out = dot(dec_t[...], grad, 1, 0)
    send[...] = out[: HID // 2].astype(BF)
    keep[...] = out[HID // 2 :].astype(BF)


def encoder_kernel(
    scal, dest, og, wd, x, we, q_ref, expand, latent_w, bh, small, packed, back_acc, pre_acc, spread, lat, count
):
    step = pl.program_id(0)

    @pl.when(step == 0)
    def _():
        back_acc[...] = jnp.zeros_like(back_acc)
        pre_acc[...] = jnp.zeros_like(pre_acc)

    back_acc[...] += dot(og[...], wd[...], 1, 1)
    pre_acc[...] += dot(x[...], we[...], 1, 0)

    @pl.when(step == STEPS - 1)
    def _():
        q = q_ref[...]
        pre_hidden = pre_acc[...]
        hidden_slope = slope_of(pre_hidden)
        hidden = jnp.where(pre_hidden > 0, pre_hidden, hidden_slope - 1.0).astype(BF)
        latents = dot(hidden, latent_w[...], 1, 0)
        lat[...] = latents
        back = (back_acc[...] * slope_of(dot(q, expand[...], 1, 1))).astype(BF)
        grad = dot(back, expand[...], 1, 0) + double_weight(scal) * (latents - q.astype(F32))
        grad = grad.astype(BF)
        bh[...] = (dot(grad, latent_w[...], 1, 1) * hidden_slope).astype(BF)
        grad_latent = dot(grad, hidden, 0, 0).T.astype(BF)
        grad_expand = dot(q, back, 0, 0).T.astype(BF)
        both = jnp.concatenate([grad_latent, grad_expand], axis=0)
        row = iota((ROWS, 1), 0)
        source = row % 8 // 4 * HID + dest_of(row // 8, scal) * 4 + row % 4
        hot = (iota((ROWS, ROWS), 1) == source).astype(BF)
        small[...] = dot(hot, both, 1, 0).reshape(128, 8, LAT).astype(BF)

        spread[...] = jnp.zeros_like(spread)
        for peer in range(PEERS):
            count[peer] = 0

        def place(slot, _):
            target = dest[slot]

            @pl.when(target >= 0)
            def _():
                rank = count[target]
                count[target] = rank + 1
                block = lat[pl.ds(pl.multiple_of(slot * BLK, BLK), BLK), :]
                spread[target, pl.ds(pl.multiple_of(rank * BLK, BLK), BLK), :] = block
                mark = jnp.full((8, LAT), dest[NB + slot] + 1, jnp.int32).astype(F32)
                spot = iota((8, LAT), 0) == rank
                old = spread[target, 2 * BLK : META, :]
                spread[target, 2 * BLK : META, :] = jnp.where(spot, mark, old)

            return 0

        lax.fori_loop(0, NB, place, 0)
        packed[...] = spread[...].astype(BF)


def outer_kernel(scal, x, bh, small_send, small_keep, send, keep):
    out = dot(x[...], bh[...], 0, 0).astype(BF)
    mine = scal[C] == 0
    low, high = out[:128], out[128:]
    for half, ref, extra in (
        (jnp.where(mine, high, low), send, small_send),
        (jnp.where(mine, low, high), keep, small_keep),
    ):
        for depth in range(4):
            spot = (depth + 4 - scal[Z]) % 4
            for part in range(4):
                ref[spot, 32 * part : 32 * part + 32, :] = half[
                    32 * depth : 32 * depth + 32, 128 * part : 128 * part + 128
                ]
        ref[:, 128:DROWS, :] = extra[...]


def arrive_kernel(got, out):
    first = got[:, 2 * BLK, :].astype(F32)
    second = got[:, 2 * BLK + 1, :].astype(F32)
    want = (iota((PEERS, LAT), 1) + 1).astype(F32)
    hot_a = (first == want).astype(F32)[:, :RB].astype(BF)
    hot_b = (second == want).astype(F32)[:, :RB].astype(BF)
    for row in range(BLK):
        out[:, row, :] = dot(hot_a, got[:, row, :], 0, 0) + dot(hot_b, got[:, BLK + row, :], 0, 0)


def decode(scal, codes, codebook, expand, x, wd):
    whole = lambda shape: pl.BlockSpec(shape, lambda i, s: (0,) * len(shape))
    return pl.pallas_call(
        decoder_kernel,
        grid_spec=pltpu.PrefetchScalarGridSpec(
            num_scalar_prefetch=1,
            grid=(STEPS,),
            in_specs=[
                whole((1, ROWS)),
                whole((CODES, LAT)),
                whole((HID, LAT)),
                pl.BlockSpec((ROWS, TILE), lambda i, s: (0, i)),
                pl.BlockSpec((HID, TILE), lambda i, s: (0, i)),
            ],
            out_specs=[
                pl.BlockSpec((ROWS, TILE), lambda i, s: (0, i)),
                pl.BlockSpec((HID // 2, TILE), lambda i, s: (0, i)),
                pl.BlockSpec((HID // 2, TILE), lambda i, s: (0, i)),
                whole((ROWS, LAT)),
            ],
            scratch_shapes=[
                pltpu.VMEM((ROWS, HID), BF),
                pltpu.VMEM((HID, ROWS), BF),
                pltpu.VMEM((ROWS, 1), F32),
            ],
        ),
        out_shape=[
            jax.ShapeDtypeStruct((ROWS, FEAT), BF),
            jax.ShapeDtypeStruct((HID // 2, FEAT), BF),
            jax.ShapeDtypeStruct((HID // 2, FEAT), BF),
            jax.ShapeDtypeStruct((ROWS, LAT), BF),
        ],
        compiler_params=pltpu.CompilerParams(vmem_limit_bytes=40 << 20),
        cost_estimate=pl.CostEstimate(flops=9 * 10**9, bytes_accessed=24 << 20, transcendentals=0),
        name="decoder_grads",
    )(scal, codes, codebook, expand, x, wd)


def encode(scal, dest, og, wd, x, we, q, expand, latent_w):
    whole = lambda shape: pl.BlockSpec(shape, lambda i, s, d: (0,) * len(shape))
    return pl.pallas_call(
        encoder_kernel,
        grid_spec=pltpu.PrefetchScalarGridSpec(
            num_scalar_prefetch=2,
            grid=(STEPS,),
            in_specs=[
                pl.BlockSpec((ROWS, TILE), lambda i, s, d: (0, i)),
                pl.BlockSpec((HID, TILE), lambda i, s, d: (0, i)),
                pl.BlockSpec((ROWS, TILE), lambda i, s, d: (0, i)),
                pl.BlockSpec((TILE, HID), lambda i, s, d: (i, 0)),
                whole((ROWS, LAT)),
                whole((HID, LAT)),
                whole((HID, LAT)),
            ],
            out_specs=[whole((ROWS, HID)), whole((128, 8, LAT)), whole((PEERS, META, LAT))],
            scratch_shapes=[
                pltpu.VMEM((ROWS, HID), F32),
                pltpu.VMEM((ROWS, HID), F32),
                pltpu.VMEM((PEERS, META, LAT), F32),
                pltpu.VMEM((ROWS, LAT), F32),
                pltpu.SMEM((PEERS,), jnp.int32),
            ],
        ),
        out_shape=[
            jax.ShapeDtypeStruct((ROWS, HID), BF),
            jax.ShapeDtypeStruct((128, 8, LAT), BF),
            jax.ShapeDtypeStruct((PEERS, META, LAT), BF),
        ],
        compiler_params=pltpu.CompilerParams(vmem_limit_bytes=48 << 20),
        cost_estimate=pl.CostEstimate(flops=11 * 10**9, bytes_accessed=24 << 20, transcendentals=0),
        name="hidden_grads",
    )(scal, dest, og, wd, x, we, q, expand, latent_w)


def outer(scal, x, bh, small):
    def near(i, s):
        return i

    def swapped(i):
        return i % 4 * 4 + i // 4

    send_at = lambda i, s: jnp.where(s[C] == 0, swapped(i), i)
    keep_at = lambda i, s: jnp.where(s[C] == 0, i, swapped(i))
    x_at = lambda i, s: (s[X] + i // 4) % 4 * 4 + (s[Y] + i % 4) % 4
    return pl.pallas_call(
        outer_kernel,
        grid_spec=pltpu.PrefetchScalarGridSpec(
            num_scalar_prefetch=1,
            grid=(16,),
            in_specs=[
                pl.BlockSpec((ROWS, 256), lambda i, s: (0, x_at(i, s))),
                pl.BlockSpec((ROWS, HID), lambda i, s: (0, 0)),
                pl.BlockSpec((4, 8, LAT), lambda i, s: (send_at(i, s), 0, 0)),
                pl.BlockSpec((4, 8, LAT), lambda i, s: (16 + keep_at(i, s), 0, 0)),
            ],
            out_specs=[
                pl.BlockSpec((4, DROWS, LAT), lambda i, s: (send_at(i, s), 0, 0)),
                pl.BlockSpec((4, DROWS, LAT), lambda i, s: (keep_at(i, s), 0, 0)),
            ],
        ),
        out_shape=[jax.ShapeDtypeStruct((64, DROWS, LAT), BF)] * 2,
        compiler_params=pltpu.CompilerParams(vmem_limit_bytes=40 << 20),
        cost_estimate=pl.CostEstimate(flops=43 * 10**8, bytes_accessed=12 << 20, transcendentals=0),
        name="encoder_grads",
    )(scal, x, bh, small, small)


def arrive(got):
    return pl.pallas_call(
        arrive_kernel,
        out_shape=jax.ShapeDtypeStruct((RB, BLK, LAT), F32),
        name="place_latents",
    )(got)


def device(col, row, core, depth):
    return ((col * 4 + row) * 2 + core) * 4 + depth


def moves(change):
    return [
        (device(x, y, c, z), device(*change(x, y, c, z)))
        for x in range(4)
        for y in range(4)
        for c in range(2)
        for z in range(4)
    ]


def turn(phase, by):
    def change(x, y, c, z):
        if phase == 2:
            return x, y, c, (z + by) % 4
        if (phase == 0) == (c == 0):
            return (x + by) % 4, y, c, z
        return x, (y + by) % 4, c, z

    return moves(change)


BOTH = ("dp", "rep")


def reduce_scatter(send, keep):
    got = lax.ppermute(send, BOTH, moves(lambda x, y, c, z: (x, y, 1 - c, z)))
    total = keep.astype(F32) + got.astype(F32)
    for phase in range(3):
        size = total.shape[0] // 4
        arrived = [
            lax.ppermute(total[by * size : (by + 1) * size].astype(BF), BOTH, turn(phase, by))
            for by in (2, 1, 3)
        ]
        total = total[:size]
        for piece in arrived:
            total = total + piece.astype(F32)
    return total


def per_device(
    frames,
    clip_lengths,
    block_dest,
    frame_codes,
    codebook,
    encoder_weight,
    latent_weight,
    expand_weight,
    decoder_weight,
):
    dp, rep = lax.axis_index("dp"), lax.axis_index("rep")
    scal = jnp.concatenate(
        [clip_lengths.reshape(4), jnp.stack([dp // 8, dp // 2 % 4, dp % 2, rep]).astype(jnp.int32)]
    )
    x = frames.reshape(ROWS, FEAT)
    og, send, keep, q = decode(
        scal, frame_codes.reshape(1, ROWS), codebook, expand_weight, x, decoder_weight
    )
    grad_decoder = reduce_scatter(send, keep)
    bh, small, packed = encode(
        scal, block_dest.reshape(2 * NB), og, decoder_weight, x, encoder_weight, q, expand_weight, latent_weight
    )
    latents = arrive(lax.all_to_all(packed, "dp", 0, 0, tiled=True))
    send, keep = outer(scal, x, bh, small)
    total = reduce_scatter(send, keep)[0]
    grad_encoder = jnp.concatenate([total[32 * part : 32 * part + 32] for part in range(4)], axis=1)
    return latents[:, None], grad_encoder, total[128:132], total[132:136], grad_decoder


def solution(mesh):
    in_specs = (
        P("dp", "rep", None, None),
        P("dp", "rep", None),
        P("dp", "rep", None, None),
        P("dp", "rep", None),
        P(),
        P(),
        P(),
        P(),
        P(),
    )
    out_specs = (P("dp", "rep", None, None),) + (P(("dp", "rep"), None),) * 4
    return jax.shard_map(
        per_device, mesh=mesh, in_specs=in_specs, out_specs=out_specs, check_vma=False
    )
```

```python
import functools

import jax
import jax.numpy as jnp
from jax import lax
from jax.experimental import pallas as pl
from jax.experimental.pallas import tpu as pltpu
from jax.sharding import PartitionSpec as P

BLK = 16
NB = 64
RB = 32
FEAT = 4096
HID = 512
LAT = 128
CODES = 1024
ROWS = NB * BLK
PEERS = 32
META = 2 * BLK + 8
DROWS = 136
JROWS = DROWS + 128
TILE = 512
STEPS = FEAT // TILE
BF = jnp.bfloat16
F32 = jnp.float32
X, Y, C, Z = range(4)


def dot(left, right, lc, rc):
    return lax.dot_general(left, right, (((lc,), (rc,)), ((), ())), preferred_element_type=F32)


def slope_of(values):
    return jnp.exp(jnp.minimum(values, 0.0))


def iota(shape, dim):
    return lax.broadcasted_iota(jnp.int32, shape, dim)


def place_of_device():
    dp = lax.axis_index("dp")
    return dp >> 3, dp >> 1 & 3, dp & 1, lax.axis_index("rep")


def double_weight(lengths):
    position = iota((ROWS, 1), 0)
    weight = jnp.zeros((ROWS, 1), F32)
    start = 0
    for clip in range(4):
        length = lengths[clip]
        span = (length + (BLK - 1)) // BLK * BLK
        inside = (position >= start) & (position < start + length)
        share = 2.0 / jnp.full((ROWS, 1), length, jnp.int32).astype(F32)
        weight = jnp.where(inside, share, weight)
        start = start + span
    return weight


def dest_of(rank, scal):
    first, second = rank >> 4, rank >> 2
    core = (1 - (rank >> 6)) ^ scal[C]
    near = 1 + 2 * core
    far = 3 - 2 * core
    col = scal[X] ^ ((first >> 1 & 1) * near) ^ ((second >> 1 & 1) * far)
    row = scal[Y] ^ ((first & 1) * near) ^ ((second & 1) * far)
    return ((col * 4 + row) * 2 + core) * 4 + ((scal[Z] + rank) & 3)


def main_kernel(
    lengths, codes, codebook, expand, latent_w, x, wd, we,
    send, keep, bh, lat, small,
    q_s, decoded, dec_t, w2, back_acc, pre_acc, order,
):
    step = pl.program_id(0)
    scal = place_of_device()

    @pl.when(step == 0)
    def _():
        by_slot = codes[:, 0, :]
        spread = (iota((BLK, ROWS), 1) & (BLK - 1) == iota((BLK, ROWS), 0)).astype(BF)
        high = dot((by_slot >> 5).astype(F32).astype(BF), spread, 1, 0)
        low = dot((by_slot & 31).astype(F32).astype(BF), spread, 1, 0)
        mine = iota((NB, ROWS), 1) >> 4 == iota((NB, ROWS), 0)
        row = jnp.sum(jnp.where(mine, high * 32.0 + low, 0.0), axis=0, keepdims=True).astype(jnp.int32)
        hot = (iota((CODES, ROWS), 0) == row).astype(BF)
        q_t = dot(codebook[...], hot, 0, 0).astype(BF)
        q = q_t.astype(F32).T.astype(BF)
        q_s[...] = q
        pre = dot(q, expand[...], 1, 1)
        decoded[...] = jnp.where(pre > 0, pre, slope_of(pre) - 1.0).astype(BF)
        source = iota((HID, 1), 0)
        source = dest_of(source >> 2, scal) * 4 + (source & 3)
        order[...] = (iota((HID, HID), 1) == source).astype(BF)
        moved = dot(order[...], expand[...], 1, 0).astype(BF)
        pre = dot(moved, q_t, 1, 0)
        dec_t[...] = jnp.where(pre > 0, pre, slope_of(pre) - 1.0).astype(BF)
        w2[...] = double_weight(lengths)
        back_acc[...] = jnp.zeros_like(back_acc)
        pre_acc[...] = jnp.zeros_like(pre_acc)

    restored = dot(decoded[...], wd[...], 1, 0)
    pre_acc[...] += dot(x[...], we[...], 1, 0)
    grad = (w2[...] * (restored - x[...].astype(F32))).astype(BF)
    out = dot(dec_t[...], grad, 1, 0)
    send[...] = out[: HID // 2].astype(BF)
    keep[...] = out[HID // 2 :].astype(BF)
    back_acc[...] += dot(grad, wd[...], 1, 1)

    @pl.when(step == STEPS - 1)
    def _():
        q = q_s[...]
        pre_hidden = pre_acc[...]
        hidden_slope = slope_of(pre_hidden)
        hidden = jnp.where(pre_hidden > 0, pre_hidden, hidden_slope - 1.0).astype(BF)
        latents = dot(hidden, latent_w[...], 1, 0)
        lat[...] = latents
        back = (back_acc[...] * slope_of(dot(q, expand[...], 1, 1))).astype(BF)
        grad = dot(back, expand[...], 1, 0) + w2[...] * (latents - q.astype(F32))
        grad = grad.astype(BF)
        bh[...] = (dot(grad, latent_w[...], 1, 1) * hidden_slope).astype(BF)
        grad_latent = dot(grad, hidden, 0, 0).T.astype(BF)
        grad_expand = dot(q, back, 0, 0).T.astype(BF)
        grad_latent = dot(order[...], grad_latent, 1, 0)
        grad_expand = dot(order[...], grad_expand, 1, 0)
        upper = iota((8, LAT), 0) < 4
        for pair in range(64):
            left, right = grad_latent[8 * pair : 8 * pair + 8], grad_expand[8 * pair : 8 * pair + 8]
            small[2 * pair] = jnp.where(upper, left, pltpu.roll(right, 4, 0)).astype(BF)
            small[2 * pair + 1] = jnp.where(upper, pltpu.roll(left, 4, 0), right).astype(BF)


def pack_kernel(dest, lat, _, packed, spread, count):
    spread[...] = jnp.zeros_like(spread)
    for peer in range(PEERS):
        count[peer] = 0

    def place(slot, _):
        target = dest[slot]

        @pl.when(target >= 0)
        def _():
            rank = count[target]
            count[target] = rank + 1
            block = lat[pl.ds(pl.multiple_of(slot * BLK, BLK), BLK), :]
            spread[target, pl.ds(pl.multiple_of(rank * BLK, BLK), BLK), :] = block
            mark = jnp.full((8, LAT), dest[NB + slot] + 1, jnp.int32).astype(F32)
            spot = iota((8, LAT), 0) == rank
            old = spread[target, 2 * BLK : META, :]
            spread[target, 2 * BLK : META, :] = jnp.where(spot, mark, old)

        return 0

    lax.fori_loop(0, NB, place, 0)
    packed[...] = spread[...].astype(BF)


def outer_kernel(x, bh, small, send, keep):
    scal = place_of_device()
    step = pl.program_id(0)
    for half, out in ((0, send), (1, keep)):
        core = scal[C] if half else 1 - scal[C]
        near = 1 + 2 * core
        wide = [x[:, pl.ds(pl.multiple_of(256 * row + 128 * core, 128), 128)] for row in range(4)]
        grad = dot(jnp.concatenate(wide, axis=1), bh[...], 0, 0).astype(BF)

        def bits(relative):
            middle = relative == 2
            first = (middle | (relative == near)).astype(jnp.int32)
            return first, (middle | (relative == 4 - near)).astype(jnp.int32)

        col_first, col_second = bits(step ^ scal[X])
        for row in range(4):
            row_first, row_second = bits(row ^ scal[Y])
            base = ((col_first * 2 + row_first) * 4 + col_second * 2 + row_second) * 4
            for depth in range(4):
                spot = base + ((depth + 4 - scal[Z]) & 3)
                top = 128 * row + 32 * depth
                for part in range(4):
                    out[spot, 32 * part : 32 * part + 32, :] = grad[top : top + 32, 128 * part : 128 * part + 128]

    @pl.when(step == 3)
    def _():
        send[:, 128:DROWS, :] = small[:64]
        keep[:, 128:DROWS, :] = small[64:]


def join_kernel(own_e, e3, e2, e1, own_d, d3, d2, d1, own, s1, s2, s3, acc):
    total = own_e[...]
    for piece in (e3, e2, e1):
        total = total + piece[...].astype(F32)
    acc[:, :DROWS, :] = total
    upper = iota((8, LAT), 0) < 4
    for pair in range(8):
        rows = slice(8 * pair, 8 * pair + 8)
        total = own_d[rows, :]
        for piece in (d3, d2, d1):
            total = total + piece[rows, :].astype(F32)
        for cols in range(16):
            left = total[:, 256 * cols : 256 * cols + 128]
            right = total[:, 256 * cols + 128 : 256 * cols + 256]
            spot = slice(DROWS + 8 * cols, DROWS + 8 * cols + 8)
            acc[2 * pair, spot, :] = jnp.where(upper, left, pltpu.roll(right, 4, 0))
            acc[2 * pair + 1, spot, :] = jnp.where(upper, pltpu.roll(left, 4, 0), right)
    own[...] = acc[0:4]
    s1[...] = acc[4:8].astype(BF)
    s2[...] = acc[8:12].astype(BF)
    s3[...] = acc[12:16].astype(BF)


def last_kernel(own, a3, a2, a1, enc, lat, exp, dec):
    total = own[0]
    for piece in (a3, a2, a1):
        total = total + piece[0].astype(F32)
    for part in range(4):
        enc[:, 128 * part : 128 * part + 128] = total[32 * part : 32 * part + 32]
    tail = total[128:DROWS]
    lat[...] = tail[:4]
    exp[...] = tail[4:]
    for cols in range(32):
        dec[:, 128 * cols : 128 * cols + 128] = total[DROWS + 4 * cols : DROWS + 4 * cols + 4]


def arrive_kernel(got, out):
    first = got[:, 2 * BLK, :].astype(F32)
    second = got[:, 2 * BLK + 1, :].astype(F32)
    want = (iota((PEERS, LAT), 1) + 1).astype(F32)
    hot_a = (first == want).astype(F32)[:, :RB].astype(BF)
    hot_b = (second == want).astype(F32)[:, :RB].astype(BF)
    for row in range(BLK):
        out[:, row, :] = dot(hot_a, got[:, row, :], 0, 0) + dot(hot_b, got[:, BLK + row, :], 0, 0)


def whole(*shape):
    return pl.BlockSpec(shape, lambda *_: (0,) * len(shape))


def main(lengths, codes, codebook, expand, latent_w, x, wd, we):
    return pl.pallas_call(
        main_kernel,
        grid_spec=pltpu.PrefetchScalarGridSpec(
            num_scalar_prefetch=1,
            grid=(STEPS,),
            in_specs=[
                whole(NB, 1, BLK),
                whole(CODES, LAT),
                whole(HID, LAT),
                whole(HID, LAT),
                pl.BlockSpec((ROWS, TILE), lambda i, s: (0, i)),
                pl.BlockSpec((HID, TILE), lambda i, s: (0, i)),
                pl.BlockSpec((TILE, HID), lambda i, s: (i, 0)),
            ],
            out_specs=[
                pl.BlockSpec((HID // 2, TILE), lambda i, s: (0, i)),
                pl.BlockSpec((HID // 2, TILE), lambda i, s: (0, i)),
                whole(ROWS, HID),
                whole(ROWS, LAT),
                whole(128, 8, LAT),
            ],
            scratch_shapes=[
                pltpu.VMEM((ROWS, LAT), BF),
                pltpu.VMEM((ROWS, HID), BF),
                pltpu.VMEM((HID, ROWS), BF),
                pltpu.VMEM((ROWS, 1), F32),
                pltpu.VMEM((ROWS, HID), F32),
                pltpu.VMEM((ROWS, HID), F32),
                pltpu.VMEM((HID, HID), BF),
            ],
        ),
        out_shape=[
            jax.ShapeDtypeStruct((HID // 2, FEAT), BF),
            jax.ShapeDtypeStruct((HID // 2, FEAT), BF),
            jax.ShapeDtypeStruct((ROWS, HID), BF),
            jax.ShapeDtypeStruct((ROWS, LAT), F32),
            jax.ShapeDtypeStruct((128, 8, LAT), BF),
        ],
        compiler_params=pltpu.CompilerParams(vmem_limit_bytes=60 << 20),
        cost_estimate=pl.CostEstimate(flops=20 * 10**9, bytes_accessed=24 << 20, transcendentals=0),
        name="forward_and_hidden_grads",
    )(lengths, codes, codebook, expand, latent_w, x, wd, we)


def pack(dest, lat, after):
    return pl.pallas_call(
        pack_kernel,
        grid_spec=pltpu.PrefetchScalarGridSpec(
            num_scalar_prefetch=1,
            grid=(1,),
            in_specs=[whole(ROWS, LAT), pl.BlockSpec(memory_space=pl.ANY)],
            out_specs=whole(PEERS, META, LAT),
            scratch_shapes=[pltpu.VMEM((PEERS, META, LAT), F32), pltpu.SMEM((PEERS,), jnp.int32)],
        ),
        out_shape=jax.ShapeDtypeStruct((PEERS, META, LAT), BF),
        compiler_params=pltpu.CompilerParams(vmem_limit_bytes=8 << 20),
        cost_estimate=pl.CostEstimate(flops=10**6, bytes_accessed=1 << 20, transcendentals=0),
        name="pack_latents",
    )(dest, lat, after)


def outer(x, bh, small):
    return pl.pallas_call(
        outer_kernel,
        grid=(4,),
        in_specs=[
            pl.BlockSpec((ROWS, FEAT // 4), lambda i: (0, i)),
            whole(ROWS, HID),
            whole(128, 8, LAT),
        ],
        out_specs=[whole(64, DROWS, LAT)] * 2,
        out_shape=[jax.ShapeDtypeStruct((64, DROWS, LAT), BF)] * 2,
        compiler_params=pltpu.CompilerParams(vmem_limit_bytes=48 << 20),
        cost_estimate=pl.CostEstimate(flops=44 * 10**8, bytes_accessed=13 << 20, transcendentals=0),
        name="encoder_grads",
    )(x, bh, small)


def join(e_own, e_arrived, d_own, d_arrived):
    return pl.pallas_call(
        join_kernel,
        out_shape=[jax.ShapeDtypeStruct((4, JROWS, LAT), F32)] + [jax.ShapeDtypeStruct((4, JROWS, LAT), BF)] * 3,
        scratch_shapes=[pltpu.VMEM((16, JROWS, LAT), F32)],
        compiler_params=pltpu.CompilerParams(vmem_limit_bytes=16 << 20),
        cost_estimate=pl.CostEstimate(flops=10**7, bytes_accessed=6 << 20, transcendentals=0),
        name="sum_first_exchange",
    )(e_own, *e_arrived, d_own, *d_arrived)


def last(own, arrived):
    return pl.pallas_call(
        last_kernel,
        out_shape=[
            jax.ShapeDtypeStruct((32, HID), F32),
            jax.ShapeDtypeStruct((4, LAT), F32),
            jax.ShapeDtypeStruct((4, LAT), F32),
            jax.ShapeDtypeStruct((4, FEAT), F32),
        ],
        compiler_params=pltpu.CompilerParams(vmem_limit_bytes=4 << 20),
        cost_estimate=pl.CostEstimate(flops=10**6, bytes_accessed=1 << 20, transcendentals=0),
        name="sum_last_exchange",
    )(own, *arrived)


def arrive(got):
    return pl.pallas_call(
        arrive_kernel,
        out_shape=jax.ShapeDtypeStruct((RB, BLK, LAT), F32),
        compiler_params=pltpu.CompilerParams(vmem_limit_bytes=4 << 20),
        cost_estimate=pl.CostEstimate(flops=10**6, bytes_accessed=1 << 20, transcendentals=0),
        name="place_latents",
    )(got)


def device(col, row, core, depth):
    return ((col * 4 + row) * 2 + core) * 4 + depth


def moves(change):
    return [
        (device(x, y, c, z), device(*change(x, y, c, z)))
        for x in range(4)
        for y in range(4)
        for c in range(2)
        for z in range(4)
    ]


BOTH = ("dp", "rep")


def flip(phase, by):
    def change(x, y, c, z):
        mask = 1 if (phase == 0) == (c == 0) else 3
        return x ^ (by // 2 * mask), y ^ (by % 2 * mask), c, z

    return moves(change)


def turn(by):
    return moves(lambda x, y, c, z: (x, y, c, (z + by) % 4))


def swap_cores(array):
    return lax.ppermute(array, BOTH, moves(lambda x, y, c, z: (x, y, 1 - c, z)))


def first_shares(keep, swap, size):
    def part(first):
        rows = slice(first * size, first * size + size)
        return keep[rows].astype(F32) + swap[rows].astype(F32)

    return part(0), [part(first).astype(BF) for first in (3, 2, 1)]


def per_device(
    frames,
    clip_lengths,
    block_dest,
    frame_codes,
    codebook,
    encoder_weight,
    latent_weight,
    expand_weight,
    decoder_weight,
):
    x = frames.reshape(ROWS, FEAT)
    send, keep, bh, lat, small = main(
        clip_lengths.reshape(4), frame_codes, codebook, expand_weight, latent_weight, x, decoder_weight, encoder_weight
    )
    d_swap = swap_cores(send)
    e_send, e_keep = outer(x, bh, small)
    e_swap = swap_cores(e_send)

    d_own, d_shares = first_shares(keep, d_swap, 64)
    d_arrived = [lax.ppermute(share, BOTH, flip(0, first)) for share, first in zip(d_shares, (3, 2, 1))]
    e_own, e_shares = first_shares(e_keep, e_swap, 16)
    e_arrived = [lax.ppermute(share, BOTH, flip(0, first)) for share, first in zip(e_shares, (3, 2, 1))]
    packed = pack(block_dest.reshape(2 * NB), lat, e_shares[0])
    got = lax.all_to_all(packed, "dp", 0, 0, tiled=True)

    own, *shares = join(e_own, e_arrived, d_own, d_arrived)
    shares, got = lax.optimization_barrier((shares, got))
    arrived = [lax.ppermute(shares[by - 1], BOTH, flip(1, by)) for by in (3, 2, 1)]
    latents = arrive(got)
    for piece in arrived:
        own = own + piece.astype(F32)
    arrived = [lax.ppermute(own[by : by + 1].astype(BF), BOTH, turn(by)) for by in (2, 3, 1)]
    grad_encoder, grad_latent, grad_expand, grad_decoder = last(own[:1], arrived)
    return latents[:, None], grad_encoder, grad_latent, grad_expand, grad_decoder


def solution(mesh):
    in_specs = (
        P("dp", "rep", None, None),
        P("dp", "rep", None),
        P("dp", "rep", None, None),
        P("dp", "rep", None),
        P(),
        P(),
        P(),
        P(),
        P(),
    )
    out_specs = (P("dp", "rep", None, None),) + (P(("dp", "rep"), None),) * 4
    return jax.shard_map(
        per_device, mesh=mesh, in_specs=in_specs, out_specs=out_specs, check_vma=False
    )
```

```python
import functools

import jax
import jax.numpy as jnp
from jax import lax
from jax.experimental import pallas as pl
from jax.experimental.pallas import tpu as pltpu
from jax.sharding import PartitionSpec as P

BLK = 16
NB = 64
RB = 32
FEAT = 4096
HID = 512
LAT = 128
CODES = 1024
USED = 60
ROWS = USED * BLK
PEERS = 32
META = 2 * BLK + 8
DROWS = 136
JROWS = DROWS + 128
TILE = 512
STEPS = FEAT // TILE
BF = jnp.bfloat16
F32 = jnp.float32
X, Y, C, Z = range(4)


def dot(left, right, lc, rc):
    return lax.dot_general(left, right, (((lc,), (rc,)), ((), ())), preferred_element_type=F32)


def slope_of(values):
    return jnp.exp(jnp.minimum(values, 0.0))


def iota(shape, dim):
    return lax.broadcasted_iota(jnp.int32, shape, dim)


def place_of_device():
    dp = lax.axis_index("dp")
    return dp >> 3, dp >> 1 & 3, dp & 1, lax.axis_index("rep")


def double_weight(lengths):
    position = iota((ROWS, 1), 0)
    weight = jnp.zeros((ROWS, 1), F32)
    start = 0
    for clip in range(4):
        length = lengths[clip]
        span = (length + (BLK - 1)) // BLK * BLK
        inside = (position >= start) & (position < start + length)
        share = 2.0 / jnp.full((ROWS, 1), length, jnp.int32).astype(F32)
        weight = jnp.where(inside, share, weight)
        start = start + span
    return weight


def dest_of(rank, scal):
    first, second = rank >> 4, rank >> 2
    core = (1 - (rank >> 6)) ^ scal[C]
    near = 1 + 2 * core
    far = 3 - 2 * core
    col = scal[X] ^ ((first >> 1 & 1) * near) ^ ((second >> 1 & 1) * far)
    row = scal[Y] ^ ((first & 1) * near) ^ ((second & 1) * far)
    return ((col * 4 + row) * 2 + core) * 4 + ((scal[Z] + rank) & 3)


def hidden_of(row, scal):
    rank = row >> 2
    core = (1 - (rank >> 6)) ^ scal[C]
    near = 1 + 2 * core
    far = 3 - 2 * core
    depth = scal[Z] ^ ((rank >> 5 & 1) * near) ^ ((rank >> 4 & 1) * far)
    col = scal[X] ^ ((rank >> 3 & 1) * far) ^ ((rank >> 1 & 1) * near)
    line = scal[Y] ^ ((rank >> 2 & 1) * far) ^ ((rank & 1) * near)
    return ((((col * 4 + line) * 2 + core) * 4 + depth) << 2) + (row & 3)


def main_kernel(
    lengths, codes, codebook, expand, latent_w, x, wd, we,
    send, keep, bh, lat, small_keep, e_send,
    q_s, decoded, dec_t, w2, back_acc, pre_acc, order, frames, small,
):
    step = pl.program_id(0)
    scal = place_of_device()

    @pl.when(step == 0)
    def _():
        by_slot = codes[:USED, 0, :]
        spread = (iota((BLK, ROWS), 1) & (BLK - 1) == iota((BLK, ROWS), 0)).astype(BF)
        high = dot((by_slot >> 5).astype(F32).astype(BF), spread, 1, 0)
        low = dot((by_slot & 31).astype(F32).astype(BF), spread, 1, 0)
        mine = iota((USED, ROWS), 1) >> 4 == iota((USED, ROWS), 0)
        row = jnp.sum(jnp.where(mine, high * 32.0 + low, 0.0), axis=0, keepdims=True).astype(jnp.int32)
        hot = (iota((CODES, ROWS), 0) == row).astype(BF)
        q_t = dot(codebook[...], hot, 0, 0).astype(BF)
        q = q_t.astype(F32).T.astype(BF)
        q_s[...] = q
        pre = dot(q, expand[...], 1, 1)
        decoded[...] = jnp.where(pre > 0, pre, slope_of(pre) - 1.0).astype(BF)
        row = iota((HID, 1), 0)
        order[...] = (iota((HID, HID), 1) == dest_of(row >> 2, scal) * 4 + (row & 3)).astype(BF)
        moved = (iota((HID, HID), 1) == hidden_of(row, scal)).astype(BF)
        moved = dot(moved, expand[...], 1, 0).astype(BF)
        pre = dot(moved, q_t, 1, 0)
        dec_t[...] = jnp.where(pre > 0, pre, slope_of(pre) - 1.0).astype(BF)
        w2[...] = double_weight(lengths)
        back_acc[...] = jnp.zeros_like(back_acc)
        pre_acc[...] = jnp.zeros_like(pre_acc)

    @pl.when(step < STEPS)
    def _():
        frames[:, pl.ds(pl.multiple_of(step * TILE, TILE), TILE)] = x[...]
        restored = dot(decoded[...], wd[...], 1, 0)
        pre_acc[...] += dot(x[...], we[...], 1, 0)
        grad = (w2[...] * (restored - x[...].astype(F32))).astype(BF)
        out = dot(dec_t[...], grad, 1, 0)
        send[...] = out[: HID // 2].astype(BF)
        keep[...] = out[HID // 2 :].astype(BF)
        back_acc[...] += dot(grad, wd[...], 1, 1)

    @pl.when(step == STEPS - 1)
    def _():
        q = q_s[...]
        pre_hidden = pre_acc[...]
        hidden_slope = slope_of(pre_hidden)
        hidden = jnp.where(pre_hidden > 0, pre_hidden, hidden_slope - 1.0).astype(BF)
        latents = dot(hidden, latent_w[...], 1, 0)
        lat[...] = latents
        back = (back_acc[...] * slope_of(dot(q, expand[...], 1, 1))).astype(BF)
        grad = dot(back, expand[...], 1, 0) + w2[...] * (latents - q.astype(F32))
        grad = grad.astype(BF)
        bh[...] = (dot(grad, latent_w[...], 1, 1) * hidden_slope).astype(BF)
        grad_latent = dot(grad, hidden, 0, 0).T.astype(BF)
        grad_expand = dot(q, back, 0, 0).T.astype(BF)
        grad_latent = dot(order[...], grad_latent, 1, 0)
        grad_expand = dot(order[...], grad_expand, 1, 0)
        upper = iota((8, LAT), 0) < 4
        for pair in range(64):
            left, right = grad_latent[8 * pair : 8 * pair + 8], grad_expand[8 * pair : 8 * pair + 8]
            small[2 * pair] = jnp.where(upper, left, pltpu.roll(right, 4, 0)).astype(BF)
            small[2 * pair + 1] = jnp.where(upper, pltpu.roll(left, 4, 0), right).astype(BF)
        small_keep[...] = small[64:]

    @pl.when(step >= STEPS)
    def _():
        first = step - STEPS
        wide = [
            frames[:, pl.ds(pl.multiple_of(dest_of(first * 16 + second * 4, scal) // 4 * 128, 128), 128)]
            for second in range(4)
        ]
        grad = dot(jnp.concatenate(wide, axis=1), bh[...], 0, 0).astype(BF)
        for second in range(4):
            for depth in range(4):
                spot = second * 4 + ((depth + 4 - scal[Z]) & 3)
                top = 128 * second + 32 * depth
                for part in range(4):
                    e_send[spot, 32 * part : 32 * part + 32, :] = grad[top : top + 32, 128 * part : 128 * part + 128]
        e_send[:, 128:DROWS, :] = small[pl.ds(first * 16, 16)]


def pack_kernel(dest, lat, _, packed, spread, count):
    spread[...] = jnp.zeros_like(spread)
    for peer in range(PEERS):
        count[peer] = 0

    def place(slot, _):
        target = dest[slot]

        @pl.when(target >= 0)
        def _():
            rank = count[target]
            count[target] = rank + 1
            block = lat[pl.ds(pl.multiple_of(slot * BLK, BLK), BLK), :]
            spread[target, pl.ds(pl.multiple_of(rank * BLK, BLK), BLK), :] = block
            mark = jnp.full((8, LAT), dest[NB + slot] + 1, jnp.int32).astype(F32)
            spot = iota((8, LAT), 0) == rank
            old = spread[target, 2 * BLK : META, :]
            spread[target, 2 * BLK : META, :] = jnp.where(spot, mark, old)

        return 0

    lax.fori_loop(0, USED, place, 0)
    packed[...] = spread[...].astype(BF)


def outer_kernel(x, bh, small, out):
    step = pl.program_id(0)
    scal = place_of_device()
    core = scal[C]
    near = 1 + 2 * core
    wide = [x[:, pl.ds(pl.multiple_of(256 * row + 128 * core, 128), 128)] for row in range(4)]
    grad = dot(jnp.concatenate(wide, axis=1), bh[...], 0, 0).astype(BF)

    def bits(relative):
        middle = relative == 2
        first = (middle | (relative == near)).astype(jnp.int32)
        return first, (middle | (relative == 4 - near)).astype(jnp.int32)

    col_first, col_second = bits(step ^ scal[X])
    for row in range(4):
        row_first, row_second = bits(row ^ scal[Y])
        base = ((col_first * 2 + row_first) * 4 + col_second * 2 + row_second) * 4
        for depth in range(4):
            spot = base + ((depth + 4 - scal[Z]) & 3)
            top = 128 * row + 32 * depth
            for part in range(4):
                out[spot, 32 * part : 32 * part + 32, :] = grad[top : top + 32, 128 * part : 128 * part + 128]

    @pl.when(step == 3)
    def _():
        out[:, 128:DROWS, :] = small[...]


def join_kernel(own_e, e3, e2, e1, own_d, d_far, own, s1, s2, s3, acc):
    total = own_e[...]
    for piece in (e3, e2, e1):
        total = total + piece[...].astype(F32)
    acc[:, :DROWS, :] = total
    upper = iota((8, LAT), 0) < 4
    for pair in range(8):
        rows = slice(8 * pair, 8 * pair + 8)
        total = own_d[rows, :] + d_far[rows, :].astype(F32)
        for cols in range(16):
            left = total[:, 256 * cols : 256 * cols + 128]
            right = total[:, 256 * cols + 128 : 256 * cols + 256]
            spot = slice(DROWS + 8 * cols, DROWS + 8 * cols + 8)
            acc[2 * pair, spot, :] = jnp.where(upper, left, pltpu.roll(right, 4, 0))
            acc[2 * pair + 1, spot, :] = jnp.where(upper, pltpu.roll(left, 4, 0), right)
    own[...] = acc[0:4]
    s1[...] = acc[4:8].astype(BF)
    s2[...] = acc[8:12].astype(BF)
    s3[...] = acc[12:16].astype(BF)


def last_kernel(own, e3, e2, e1, d3, d2, d1, enc, lat, exp, dec):
    total = own[0, :DROWS, :]
    for piece in (e3, e2, e1):
        total = total + piece[0].astype(F32)
    for part in range(4):
        enc[:, 128 * part : 128 * part + 128] = total[32 * part : 32 * part + 32]
    tail = total[128:DROWS]
    lat[...] = tail[:4]
    exp[...] = tail[4:]
    total = own[0, DROWS:, :]
    for piece in (d3, d2, d1):
        total = total + piece[0].astype(F32)
    for cols in range(32):
        dec[:, 128 * cols : 128 * cols + 128] = total[4 * cols : 4 * cols + 4]


def arrive_kernel(got, out):
    first = got[:, 2 * BLK, :].astype(F32)
    second = got[:, 2 * BLK + 1, :].astype(F32)
    want = (iota((PEERS, LAT), 1) + 1).astype(F32)
    hot_a = (first == want).astype(F32)[:, :RB].astype(BF)
    hot_b = (second == want).astype(F32)[:, :RB].astype(BF)
    for row in range(BLK):
        out[:, row, :] = dot(hot_a, got[:, row, :], 0, 0) + dot(hot_b, got[:, BLK + row, :], 0, 0)


def whole(*shape):
    return pl.BlockSpec(shape, lambda *_: (0,) * len(shape))


def main(lengths, codes, codebook, expand, latent_w, x, wd, we):
    columns = lambda i, s: (0, jnp.minimum(i, STEPS - 1))
    return pl.pallas_call(
        main_kernel,
        grid_spec=pltpu.PrefetchScalarGridSpec(
            num_scalar_prefetch=1,
            grid=(STEPS + 4,),
            in_specs=[
                whole(NB, 1, BLK),
                whole(CODES, LAT),
                whole(HID, LAT),
                whole(HID, LAT),
                pl.BlockSpec((ROWS, TILE), columns),
                pl.BlockSpec((HID, TILE), columns),
                pl.BlockSpec((TILE, HID), lambda i, s: (jnp.minimum(i, STEPS - 1), 0)),
            ],
            out_specs=[
                pl.BlockSpec((HID // 2, TILE), columns),
                pl.BlockSpec((HID // 2, TILE), columns),
                whole(ROWS, HID),
                whole(ROWS, LAT),
                whole(64, 8, LAT),
                pl.BlockSpec((16, DROWS, LAT), lambda i, s: (jnp.maximum(i - STEPS, 0), 0, 0)),
            ],
            scratch_shapes=[
                pltpu.VMEM((ROWS, LAT), BF),
                pltpu.VMEM((ROWS, HID), BF),
                pltpu.VMEM((HID, ROWS), BF),
                pltpu.VMEM((ROWS, 1), F32),
                pltpu.VMEM((ROWS, HID), F32),
                pltpu.VMEM((ROWS, HID), F32),
                pltpu.VMEM((HID, HID), BF),
                pltpu.VMEM((ROWS, FEAT), BF),
                pltpu.VMEM((128, 8, LAT), BF),
            ],
        ),
        out_shape=[
            jax.ShapeDtypeStruct((HID // 2, FEAT), BF),
            jax.ShapeDtypeStruct((HID // 2, FEAT), BF),
            jax.ShapeDtypeStruct((ROWS, HID), BF),
            jax.ShapeDtypeStruct((ROWS, LAT), F32),
            jax.ShapeDtypeStruct((64, 8, LAT), BF),
            jax.ShapeDtypeStruct((64, DROWS, LAT), BF),
        ],
        compiler_params=pltpu.CompilerParams(vmem_limit_bytes=60 << 20),
        cost_estimate=pl.CostEstimate(flops=20 * 10**9, bytes_accessed=24 << 20, transcendentals=0),
        name="forward_and_hidden_grads",
    )(lengths, codes, codebook, expand, latent_w, x, wd, we)


def pack(dest, lat, after):
    return pl.pallas_call(
        pack_kernel,
        grid_spec=pltpu.PrefetchScalarGridSpec(
            num_scalar_prefetch=1,
            grid=(1,),
            in_specs=[whole(ROWS, LAT), pl.BlockSpec(memory_space=pl.ANY)],
            out_specs=whole(PEERS, META, LAT),
            scratch_shapes=[pltpu.VMEM((PEERS, META, LAT), F32), pltpu.SMEM((PEERS,), jnp.int32)],
        ),
        out_shape=jax.ShapeDtypeStruct((PEERS, META, LAT), BF),
        compiler_params=pltpu.CompilerParams(vmem_limit_bytes=8 << 20),
        cost_estimate=pl.CostEstimate(flops=10**6, bytes_accessed=1 << 20, transcendentals=0),
        name="pack_latents",
    )(dest, lat, after)


def outer(x, bh, small):
    return pl.pallas_call(
        outer_kernel,
        grid=(4,),
        in_specs=[
            pl.BlockSpec((ROWS, FEAT // 4), lambda i: (0, i)),
            whole(ROWS, HID),
            whole(64, 8, LAT),
        ],
        out_specs=whole(64, DROWS, LAT),
        out_shape=jax.ShapeDtypeStruct((64, DROWS, LAT), BF),
        compiler_params=pltpu.CompilerParams(vmem_limit_bytes=48 << 20),
        cost_estimate=pl.CostEstimate(flops=22 * 10**8, bytes_accessed=11 << 20, transcendentals=0),
        name="encoder_grads",
    )(x, bh, small)


def join(e_own, e_arrived, d_own, d_far):
    return pl.pallas_call(
        join_kernel,
        out_shape=[jax.ShapeDtypeStruct((4, JROWS, LAT), F32)] + [jax.ShapeDtypeStruct((4, JROWS, LAT), BF)] * 3,
        scratch_shapes=[pltpu.VMEM((16, JROWS, LAT), F32)],
        compiler_params=pltpu.CompilerParams(vmem_limit_bytes=16 << 20),
        cost_estimate=pl.CostEstimate(flops=10**7, bytes_accessed=6 << 20, transcendentals=0),
        name="sum_first_exchange",
    )(e_own, *e_arrived, d_own, d_far)


def last(own, arrived):
    return pl.pallas_call(
        last_kernel,
        out_shape=[
            jax.ShapeDtypeStruct((32, HID), F32),
            jax.ShapeDtypeStruct((4, LAT), F32),
            jax.ShapeDtypeStruct((4, LAT), F32),
            jax.ShapeDtypeStruct((4, FEAT), F32),
        ],
        compiler_params=pltpu.CompilerParams(vmem_limit_bytes=4 << 20),
        cost_estimate=pl.CostEstimate(flops=10**6, bytes_accessed=1 << 20, transcendentals=0),
        name="sum_last_exchange",
    )(own, *arrived)


def arrive(got):
    return pl.pallas_call(
        arrive_kernel,
        out_shape=jax.ShapeDtypeStruct((RB, BLK, LAT), F32),
        compiler_params=pltpu.CompilerParams(vmem_limit_bytes=4 << 20),
        cost_estimate=pl.CostEstimate(flops=10**6, bytes_accessed=1 << 20, transcendentals=0),
        name="place_latents",
    )(got)


def device(col, row, core, depth):
    return ((col * 4 + row) * 2 + core) * 4 + depth


def moves(change):
    return [
        (device(x, y, c, z), device(*change(x, y, c, z)))
        for x in range(4)
        for y in range(4)
        for c in range(2)
        for z in range(4)
    ]


BOTH = ("dp", "rep")


def flip(phase, by):
    def change(x, y, c, z):
        mask = 1 if (phase == 0) == (c == 0) else 3
        return x ^ (by // 2 * mask), y ^ (by % 2 * mask), c, z

    return moves(change)


def flip_z(phase):
    return moves(lambda x, y, c, z: (x, y, c, z ^ (1 if (phase == 0) == (c == 0) else 3)))


def turn(by):
    return moves(lambda x, y, c, z: (x, y, c, (z + by) % 4))


def swap_cores(array):
    return lax.ppermute(array, BOTH, moves(lambda x, y, c, z: (x, y, 1 - c, z)))


def first_shares(keep, swap, size):
    def part(first):
        rows = slice(first * size, first * size + size)
        return keep[rows].astype(F32) + swap[rows].astype(F32)

    return part(0), [part(first).astype(BF) for first in (3, 2, 1)]


def per_device(
    frames,
    clip_lengths,
    block_dest,
    frame_codes,
    codebook,
    encoder_weight,
    latent_weight,
    expand_weight,
    decoder_weight,
):
    x = frames.reshape(NB * BLK, FEAT)
    send, keep, bh, lat, small, e_send = main(
        clip_lengths.reshape(4), frame_codes, codebook, expand_weight, latent_weight, x, decoder_weight, encoder_weight
    )
    d_swap = swap_cores(send)
    e_swap = swap_cores(e_send)
    e_keep = outer(x, bh, small)

    share = (keep[128:].astype(F32) + d_swap[128:].astype(F32)).astype(BF)
    d_near = lax.ppermute(share, BOTH, flip_z(0))
    d_own = keep[:128].astype(F32) + d_swap[:128].astype(F32)
    e_own, e_shares = first_shares(e_keep, e_swap, 16)
    e_arrived = [lax.ppermute(share, BOTH, flip(0, first)) for share, first in zip(e_shares, (3, 2, 1))]
    packed = pack(block_dest.reshape(2 * NB), lat, e_shares[0])
    got = lax.all_to_all(packed, "dp", 0, 0, tiled=True)

    d_far = lax.ppermute((d_own[64:] + d_near[64:].astype(F32)).astype(BF), BOTH, flip_z(1))
    d_own = d_own[:64] + d_near[:64].astype(F32)
    own, *shares = join(e_own, e_arrived, d_own, d_far)
    arrived = [lax.ppermute(shares[by - 1], BOTH, flip(1, by)) for by in (3, 2, 1)]
    arrived, got = lax.optimization_barrier((arrived, got))
    latents = arrive(got)
    for piece in arrived:
        own = own + piece.astype(F32)
    shares = own.astype(BF)
    e_arrived = [lax.ppermute(shares[by : by + 1, :DROWS], BOTH, turn(by)) for by in (2, 3, 1)]
    d_arrived = [lax.ppermute(shares[by : by + 1, DROWS:], BOTH, flip(0, by)) for by in (3, 2, 1)]
    grad_encoder, grad_latent, grad_expand, grad_decoder = last(own[:1], e_arrived + d_arrived)
    return latents[:, None], grad_encoder, grad_latent, grad_expand, grad_decoder


def solution(mesh):
    in_specs = (
        P("dp", "rep", None, None),
        P("dp", "rep", None),
        P("dp", "rep", None, None),
        P("dp", "rep", None),
        P(),
        P(),
        P(),
        P(),
        P(),
    )
    out_specs = (P("dp", "rep", None, None),) + (P(("dp", "rep"), None),) * 4
    return jax.shard_map(
        per_device, mesh=mesh, in_specs=in_specs, out_specs=out_specs, check_vma=False
    )
```

```python
import functools

import jax
import jax.numpy as jnp
from jax import lax
from jax.experimental import pallas as pl
from jax.experimental.pallas import tpu as pltpu
from jax.sharding import PartitionSpec as P

BLK = 16
NB = 64
RB = 32
FEAT = 4096
HID = 512
LAT = 128
CODES = 1024
USED = 60
ROWS = USED * BLK
PEERS = 32
META = 2 * BLK + 8
DROWS = 136
JROWS = DROWS + 128
TILE = 1024
STEPS = FEAT // TILE
BF = jnp.bfloat16
F32 = jnp.float32
X, Y, C, Z = range(4)


def dot(left, right, lc, rc):
    return lax.dot_general(left, right, (((lc,), (rc,)), ((), ())), preferred_element_type=F32)


def slope_of(values):
    return jnp.exp(jnp.minimum(values, 0.0))


def iota(shape, dim):
    return lax.broadcasted_iota(jnp.int32, shape, dim)


def place_of_device():
    dp = lax.axis_index("dp")
    return dp >> 3, dp >> 1 & 3, dp & 1, lax.axis_index("rep")


def double_weight(lengths):
    position = iota((ROWS, 1), 0)
    weight = jnp.zeros((ROWS, 1), F32)
    start = 0
    for clip in range(4):
        length = lengths[clip]
        span = (length + (BLK - 1)) // BLK * BLK
        inside = (position >= start) & (position < start + length)
        share = 2.0 / jnp.full((ROWS, 1), length, jnp.int32).astype(F32)
        weight = jnp.where(inside, share, weight)
        start = start + span
    return weight


def dest_of(rank, scal):
    first, second = rank >> 4, rank >> 2
    core = (1 - (rank >> 6)) ^ scal[C]
    near = 1 + 2 * core
    far = 3 - 2 * core
    col = scal[X] ^ ((first >> 1 & 1) * near) ^ ((second >> 1 & 1) * far)
    row = scal[Y] ^ ((first & 1) * near) ^ ((second & 1) * far)
    return ((col * 4 + row) * 2 + core) * 4 + ((scal[Z] + rank) & 3)


def hidden_of(row, scal):
    rank = row >> 2
    core = (1 - (rank >> 6)) ^ scal[C]
    near = 1 + 2 * core
    far = 3 - 2 * core
    depth = scal[Z] ^ ((rank >> 5 & 1) * near) ^ ((rank >> 4 & 1) * far)
    col = scal[X] ^ ((rank >> 3 & 1) * far) ^ ((rank >> 1 & 1) * near)
    line = scal[Y] ^ ((rank >> 2 & 1) * far) ^ ((rank & 1) * near)
    return ((((col * 4 + line) * 2 + core) * 4 + depth) << 2) + (row & 3)


def main_kernel(
    lengths, codes, codebook, expand, latent_w, x, wd, we,
    send, keep, bh, lat, small_keep, e_send,
    q_s, decoded, dec_t, w2, back_acc, pre_acc, order, frames, small,
):
    step = pl.program_id(0)
    scal = place_of_device()

    @pl.when(step == 0)
    def _():
        by_slot = codes[:USED, 0, :]
        spread = (iota((BLK, ROWS), 1) & (BLK - 1) == iota((BLK, ROWS), 0)).astype(BF)
        high = dot((by_slot >> 5).astype(F32).astype(BF), spread, 1, 0)
        low = dot((by_slot & 31).astype(F32).astype(BF), spread, 1, 0)
        mine = iota((USED, ROWS), 1) >> 4 == iota((USED, ROWS), 0)
        row = jnp.sum(jnp.where(mine, high * 32.0 + low, 0.0), axis=0, keepdims=True).astype(jnp.int32)
        hot = (iota((CODES, ROWS), 0) == row).astype(BF)
        q_t = dot(codebook[...], hot, 0, 0).astype(BF)
        q = q_t.astype(F32).T.astype(BF)
        q_s[...] = q
        pre = dot(q, expand[...], 1, 1)
        decoded[...] = jnp.where(pre > 0, pre, slope_of(pre) - 1.0).astype(BF)
        row = iota((HID, 1), 0)
        order[...] = (iota((HID, HID), 1) == dest_of(row >> 2, scal) * 4 + (row & 3)).astype(BF)
        moved = (iota((HID, HID), 1) == hidden_of(row, scal)).astype(BF)
        moved = dot(moved, expand[...], 1, 0).astype(BF)
        pre = dot(moved, q_t, 1, 0)
        dec_t[...] = jnp.where(pre > 0, pre, slope_of(pre) - 1.0).astype(BF)
        w2[...] = double_weight(lengths)
        back_acc[...] = jnp.zeros_like(back_acc)
        pre_acc[...] = jnp.zeros_like(pre_acc)

    @pl.when(step < STEPS)
    def _():
        frames[:, pl.ds(pl.multiple_of(step * TILE, TILE), TILE)] = x[...]
        restored = dot(decoded[...], wd[...], 1, 0)
        pre_acc[...] += dot(x[...], we[...], 1, 0)
        grad = (w2[...] * (restored - x[...].astype(F32))).astype(BF)
        out = dot(dec_t[...], grad, 1, 0)
        send[...] = out[: HID // 2].astype(BF)
        keep[...] = out[HID // 2 :].astype(BF)
        back_acc[...] += dot(grad, wd[...], 1, 1)

    @pl.when(step == STEPS - 1)
    def _():
        q = q_s[...]
        pre_hidden = pre_acc[...]
        hidden_slope = slope_of(pre_hidden)
        hidden = jnp.where(pre_hidden > 0, pre_hidden, hidden_slope - 1.0).astype(BF)
        latents = dot(hidden, latent_w[...], 1, 0)
        lat[...] = latents
        back = (back_acc[...] * slope_of(dot(q, expand[...], 1, 1))).astype(BF)
        grad = dot(back, expand[...], 1, 0) + w2[...] * (latents - q.astype(F32))
        grad = grad.astype(BF)
        bh[...] = (dot(grad, latent_w[...], 1, 1) * hidden_slope).astype(BF)
        grad_latent = dot(grad, hidden, 0, 0).T.astype(BF)
        grad_expand = dot(q, back, 0, 0).T.astype(BF)
        grad_latent = dot(order[...], grad_latent, 1, 0)
        grad_expand = dot(order[...], grad_expand, 1, 0)
        upper = iota((8, LAT), 0) < 4
        for pair in range(64):
            left, right = grad_latent[8 * pair : 8 * pair + 8], grad_expand[8 * pair : 8 * pair + 8]
            small[2 * pair] = jnp.where(upper, left, pltpu.roll(right, 4, 0)).astype(BF)
            small[2 * pair + 1] = jnp.where(upper, pltpu.roll(left, 4, 0), right).astype(BF)
        small_keep[...] = small[64:]

    @pl.when(step >= STEPS)
    def _():
        first = step - STEPS
        wide = [
            frames[:, pl.ds(pl.multiple_of(dest_of(first * 16 + second * 4, scal) // 4 * 128, 128), 128)]
            for second in range(4)
        ]
        grad = dot(jnp.concatenate(wide, axis=1), bh[...], 0, 0).astype(BF)
        for second in range(4):
            for depth in range(4):
                spot = second * 4 + ((depth + 4 - scal[Z]) & 3)
                top = 128 * second + 32 * depth
                for part in range(4):
                    e_send[spot, 32 * part : 32 * part + 32, :] = grad[top : top + 32, 128 * part : 128 * part + 128]
        e_send[:, 128:DROWS, :] = small[pl.ds(first * 16, 16)]


def pack_kernel(dest, lat, _, packed, spread, count):
    spread[...] = jnp.zeros_like(spread)
    for peer in range(PEERS):
        count[peer] = 0

    def place(slot, _):
        target = dest[slot]

        @pl.when(target >= 0)
        def _():
            rank = count[target]
            count[target] = rank + 1
            block = lat[pl.ds(pl.multiple_of(slot * BLK, BLK), BLK), :]
            spread[target, pl.ds(pl.multiple_of(rank * BLK, BLK), BLK), :] = block
            mark = jnp.full((8, LAT), dest[NB + slot] + 1, jnp.int32).astype(F32)
            spot = iota((8, LAT), 0) == rank
            old = spread[target, 2 * BLK : META, :]
            spread[target, 2 * BLK : META, :] = jnp.where(spot, mark, old)

        return 0

    lax.fori_loop(0, USED, place, 0)
    packed[...] = spread[...].astype(BF)


def outer_kernel(x, bh, small, out):
    step = pl.program_id(0)
    scal = place_of_device()
    core = scal[C]
    near = 1 + 2 * core
    wide = [x[:, pl.ds(pl.multiple_of(256 * row + 128 * core, 128), 128)] for row in range(4)]
    grad = dot(jnp.concatenate(wide, axis=1), bh[...], 0, 0).astype(BF)

    def bits(relative):
        middle = relative == 2
        first = (middle | (relative == near)).astype(jnp.int32)
        return first, (middle | (relative == 4 - near)).astype(jnp.int32)

    col_first, col_second = bits(step ^ scal[X])
    for row in range(4):
        row_first, row_second = bits(row ^ scal[Y])
        base = ((col_first * 2 + row_first) * 4 + col_second * 2 + row_second) * 4
        for depth in range(4):
            spot = base + ((depth + 4 - scal[Z]) & 3)
            top = 128 * row + 32 * depth
            for part in range(4):
                out[spot, 32 * part : 32 * part + 32, :] = grad[top : top + 32, 128 * part : 128 * part + 128]

    @pl.when(step == 3)
    def _():
        out[:, 128:DROWS, :] = small[...]


def join_kernel(own_e, e3, e2, e1, own_d, d_far, own, s1, s2, s3, acc):
    total = own_e[...]
    for piece in (e3, e2, e1):
        total = total + piece[...].astype(F32)
    acc[:, :DROWS, :] = total
    upper = iota((8, LAT), 0) < 4
    for pair in range(8):
        rows = slice(8 * pair, 8 * pair + 8)
        total = own_d[rows, :] + d_far[rows, :].astype(F32)
        for cols in range(16):
            left = total[:, 256 * cols : 256 * cols + 128]
            right = total[:, 256 * cols + 128 : 256 * cols + 256]
            spot = slice(DROWS + 8 * cols, DROWS + 8 * cols + 8)
            acc[2 * pair, spot, :] = jnp.where(upper, left, pltpu.roll(right, 4, 0))
            acc[2 * pair + 1, spot, :] = jnp.where(upper, pltpu.roll(left, 4, 0), right)
    own[...] = acc[0:4]
    s1[...] = acc[4:8].astype(BF)
    s2[...] = acc[8:12].astype(BF)
    s3[...] = acc[12:16].astype(BF)


def last_kernel(own, e3, e2, e1, d3, d2, d1, enc, lat, exp, dec):
    total = own[0, :DROWS, :]
    for piece in (e3, e2, e1):
        total = total + piece[0].astype(F32)
    for part in range(4):
        enc[:, 128 * part : 128 * part + 128] = total[32 * part : 32 * part + 32]
    tail = total[128:DROWS]
    lat[...] = tail[:4]
    exp[...] = tail[4:]
    total = own[0, DROWS:, :]
    for piece in (d3, d2, d1):
        total = total + piece[0].astype(F32)
    for cols in range(32):
        dec[:, 128 * cols : 128 * cols + 128] = total[4 * cols : 4 * cols + 4]


def arrive_kernel(got, out):
    first = got[:, 2 * BLK, :].astype(F32)
    second = got[:, 2 * BLK + 1, :].astype(F32)
    want = (iota((PEERS, LAT), 1) + 1).astype(F32)
    hot_a = (first == want).astype(F32)[:, :RB].astype(BF)
    hot_b = (second == want).astype(F32)[:, :RB].astype(BF)
    for row in range(BLK):
        out[:, row, :] = dot(hot_a, got[:, row, :], 0, 0) + dot(hot_b, got[:, BLK + row, :], 0, 0)


def whole(*shape):
    return pl.BlockSpec(shape, lambda *_: (0,) * len(shape))


def main(lengths, codes, codebook, expand, latent_w, x, wd, we):
    columns = lambda i, s: (0, jnp.minimum(i, STEPS - 1))
    return pl.pallas_call(
        main_kernel,
        grid_spec=pltpu.PrefetchScalarGridSpec(
            num_scalar_prefetch=1,
            grid=(STEPS + 4,),
            in_specs=[
                whole(NB, 1, BLK),
                whole(CODES, LAT),
                whole(HID, LAT),
                whole(HID, LAT),
                pl.BlockSpec((ROWS, TILE), columns),
                pl.BlockSpec((HID, TILE), columns),
                pl.BlockSpec((TILE, HID), lambda i, s: (jnp.minimum(i, STEPS - 1), 0)),
            ],
            out_specs=[
                pl.BlockSpec((HID // 2, TILE), columns),
                pl.BlockSpec((HID // 2, TILE), columns),
                whole(ROWS, HID),
                whole(ROWS, LAT),
                whole(64, 8, LAT),
                pl.BlockSpec((16, DROWS, LAT), lambda i, s: (jnp.maximum(i - STEPS, 0), 0, 0)),
            ],
            scratch_shapes=[
                pltpu.VMEM((ROWS, LAT), BF),
                pltpu.VMEM((ROWS, HID), BF),
                pltpu.VMEM((HID, ROWS), BF),
                pltpu.VMEM((ROWS, 1), F32),
                pltpu.VMEM((ROWS, HID), F32),
                pltpu.VMEM((ROWS, HID), F32),
                pltpu.VMEM((HID, HID), BF),
                pltpu.VMEM((ROWS, FEAT), BF),
                pltpu.VMEM((128, 8, LAT), BF),
            ],
        ),
        out_shape=[
            jax.ShapeDtypeStruct((HID // 2, FEAT), BF),
            jax.ShapeDtypeStruct((HID // 2, FEAT), BF),
            jax.ShapeDtypeStruct((ROWS, HID), BF),
            jax.ShapeDtypeStruct((ROWS, LAT), F32),
            jax.ShapeDtypeStruct((64, 8, LAT), BF),
            jax.ShapeDtypeStruct((64, DROWS, LAT), BF),
        ],
        compiler_params=pltpu.CompilerParams(vmem_limit_bytes=60 << 20),
        cost_estimate=pl.CostEstimate(flops=20 * 10**9, bytes_accessed=24 << 20, transcendentals=0),
        name="forward_and_hidden_grads",
    )(lengths, codes, codebook, expand, latent_w, x, wd, we)


def pack(dest, lat, after):
    return pl.pallas_call(
        pack_kernel,
        grid_spec=pltpu.PrefetchScalarGridSpec(
            num_scalar_prefetch=1,
            grid=(1,),
            in_specs=[whole(ROWS, LAT), pl.BlockSpec(memory_space=pl.ANY)],
            out_specs=whole(PEERS, META, LAT),
            scratch_shapes=[pltpu.VMEM((PEERS, META, LAT), F32), pltpu.SMEM((PEERS,), jnp.int32)],
        ),
        out_shape=jax.ShapeDtypeStruct((PEERS, META, LAT), BF),
        compiler_params=pltpu.CompilerParams(vmem_limit_bytes=8 << 20),
        cost_estimate=pl.CostEstimate(flops=10**6, bytes_accessed=1 << 20, transcendentals=0),
        name="pack_latents",
    )(dest, lat, after)


def outer(x, bh, small):
    return pl.pallas_call(
        outer_kernel,
        grid=(4,),
        in_specs=[
            pl.BlockSpec((ROWS, FEAT // 4), lambda i: (0, i)),
            whole(ROWS, HID),
            whole(64, 8, LAT),
        ],
        out_specs=whole(64, DROWS, LAT),
        out_shape=jax.ShapeDtypeStruct((64, DROWS, LAT), BF),
        compiler_params=pltpu.CompilerParams(vmem_limit_bytes=48 << 20),
        cost_estimate=pl.CostEstimate(flops=22 * 10**8, bytes_accessed=11 << 20, transcendentals=0),
        name="encoder_grads",
    )(x, bh, small)


def join(e_own, e_arrived, d_own, d_far):
    return pl.pallas_call(
        join_kernel,
        out_shape=[jax.ShapeDtypeStruct((4, JROWS, LAT), F32)] + [jax.ShapeDtypeStruct((4, JROWS, LAT), BF)] * 3,
        scratch_shapes=[pltpu.VMEM((16, JROWS, LAT), F32)],
        compiler_params=pltpu.CompilerParams(vmem_limit_bytes=16 << 20),
        cost_estimate=pl.CostEstimate(flops=10**7, bytes_accessed=6 << 20, transcendentals=0),
        name="sum_first_exchange",
    )(e_own, *e_arrived, d_own, d_far)


def last(own, arrived):
    return pl.pallas_call(
        last_kernel,
        out_shape=[
            jax.ShapeDtypeStruct((32, HID), F32),
            jax.ShapeDtypeStruct((4, LAT), F32),
            jax.ShapeDtypeStruct((4, LAT), F32),
            jax.ShapeDtypeStruct((4, FEAT), F32),
        ],
        compiler_params=pltpu.CompilerParams(vmem_limit_bytes=4 << 20),
        cost_estimate=pl.CostEstimate(flops=10**6, bytes_accessed=1 << 20, transcendentals=0),
        name="sum_last_exchange",
    )(own, *arrived)


def arrive(got):
    return pl.pallas_call(
        arrive_kernel,
        out_shape=jax.ShapeDtypeStruct((RB, BLK, LAT), F32),
        compiler_params=pltpu.CompilerParams(vmem_limit_bytes=4 << 20),
        cost_estimate=pl.CostEstimate(flops=10**6, bytes_accessed=1 << 20, transcendentals=0),
        name="place_latents",
    )(got)


def device(col, row, core, depth):
    return ((col * 4 + row) * 2 + core) * 4 + depth


def moves(change):
    return [
        (device(x, y, c, z), device(*change(x, y, c, z)))
        for x in range(4)
        for y in range(4)
        for c in range(2)
        for z in range(4)
    ]


BOTH = ("dp", "rep")


def flip(phase, by):
    def change(x, y, c, z):
        mask = 1 if (phase == 0) == (c == 0) else 3
        return x ^ (by // 2 * mask), y ^ (by % 2 * mask), c, z

    return moves(change)


def flip_z(phase):
    return moves(lambda x, y, c, z: (x, y, c, z ^ (1 if (phase == 0) == (c == 0) else 3)))


def turn(by):
    return moves(lambda x, y, c, z: (x, y, c, (z + by) % 4))


def swap_cores(array):
    return lax.ppermute(array, BOTH, moves(lambda x, y, c, z: (x, y, 1 - c, z)))


def first_shares(keep, swap, size):
    def part(first):
        rows = slice(first * size, first * size + size)
        return keep[rows].astype(F32) + swap[rows].astype(F32)

    return part(0), [part(first).astype(BF) for first in (3, 2, 1)]


def per_device(
    frames,
    clip_lengths,
    block_dest,
    frame_codes,
    codebook,
    encoder_weight,
    latent_weight,
    expand_weight,
    decoder_weight,
):
    x = frames.reshape(NB * BLK, FEAT)
    send, keep, bh, lat, small, e_send = main(
        clip_lengths.reshape(4), frame_codes, codebook, expand_weight, latent_weight, x, decoder_weight, encoder_weight
    )
    d_swap = swap_cores(send)
    e_swap = swap_cores(e_send)
    e_keep = outer(x, bh, small)

    share = (keep[128:].astype(F32) + d_swap[128:].astype(F32)).astype(BF)
    d_near = lax.ppermute(share, BOTH, flip_z(0))
    d_own = keep[:128].astype(F32) + d_swap[:128].astype(F32)
    e_own, e_shares = first_shares(e_keep, e_swap, 16)
    e_arrived = [lax.ppermute(share, BOTH, flip(0, first)) for share, first in zip(e_shares, (3, 2, 1))]
    packed = pack(block_dest.reshape(2 * NB), lat, e_shares[0])
    got = lax.all_to_all(packed, "dp", 0, 0, tiled=True)

    d_far = lax.ppermute((d_own[64:] + d_near[64:].astype(F32)).astype(BF), BOTH, flip_z(1))
    d_own = d_own[:64] + d_near[:64].astype(F32)
    own, *shares = join(e_own, e_arrived, d_own, d_far)
    arrived = [lax.ppermute(shares[by - 1], BOTH, flip(1, by)) for by in (3, 2, 1)]
    arrived, got = lax.optimization_barrier((arrived, got))
    latents = arrive(got)
    for piece in arrived:
        own = own + piece.astype(F32)
    shares = own.astype(BF)
    e_arrived = [lax.ppermute(shares[by : by + 1, :DROWS], BOTH, turn(by)) for by in (2, 3, 1)]
    d_arrived = [lax.ppermute(shares[by : by + 1, DROWS:], BOTH, flip(0, by)) for by in (3, 2, 1)]
    grad_encoder, grad_latent, grad_expand, grad_decoder = last(own[:1], e_arrived + d_arrived)
    return latents[:, None], grad_encoder, grad_latent, grad_expand, grad_decoder


def solution(mesh):
    in_specs = (
        P("dp", "rep", None, None),
        P("dp", "rep", None),
        P("dp", "rep", None, None),
        P("dp", "rep", None),
        P(),
        P(),
        P(),
        P(),
        P(),
    )
    out_specs = (P("dp", "rep", None, None),) + (P(("dp", "rep"), None),) * 4
    return jax.shard_map(
        per_device, mesh=mesh, in_specs=in_specs, out_specs=out_specs, check_vma=False
    )
```
